128 devices in a mesh: row: 8 (over y, x_lo), col: 16 (over x_hi, z, core).
Axes of the slice: x: 4 (x_hi: 2, x_lo: 2; x = x_hi * 2 + x_lo), y: 4, z: 4, core: 2. Of those that a mesh axis runs over, the one named last changes fastest.
Arguments:
- vectors: float32 [512, 32768], P(None, ('row', 'col')), may hold values from -6 to 6
- blocks: float32 [4096, 131072], P(None, ('row', 'col')), may hold values from -0.3 to 0.3
- blk_row: int32 [131072], P(('row', 'col')), may hold values from 0 to 32767, as said below
- blk_col: int32 [131072], P(('row', 'col')), may hold values from 0 to 32767, as said below
- live_counts: int32 [128], P(('row', 'col')), may hold values from 128 to 1024, as said below
Outputs:
- product: float32 [512, 32768], P(None, ('row', 'col'))
The draws below stay inside these ranges and needn't reach their ends.
Inputs may be any that keep to these rules, and one draw needn't show every extreme that they name: `blk_row`: A slot of the device at row index r and col index c has a block row in [r * size of col * 256, (r + 1) * size of col * 256). `blk_col`: A slot of the device at col index c has a block column k with (k // 256) % (size of col) == c. `live_counts`: some device has all 1024 slots live.
All inputs are finite; a program needn't handle non-finite values.
Results may differ from the reference program's by a relative error of at most 0.0003.
Values sent between devices are 32-bit elements; how exact they have to be, the bound alone decides.
A program may use at most 128 MiB of HBM per device.

```python
import jax
import jax.numpy as jnp
from jax import lax

B = 64
NV = 8
SB = 256
CAP = 1024
NB = 32768
STORED = 131072
N_ROW = 8
N_COL = 16
DEVICES = 128


def draw_blk_row(key, part):
    key = jax.random.fold_in(key, 11)
    slot_device = jnp.arange(DEVICES * CAP, dtype=jnp.int32) // CAP
    row_group = slot_device // N_COL
    inside = jax.random.randint(key, (DEVICES * CAP,), 0, N_COL * SB, dtype=jnp.int32)
    return row_group * (N_COL * SB) + inside


def draw_blk_col(key, part):
    key = jax.random.fold_in(key, 23)
    slot_device = jnp.arange(DEVICES * CAP, dtype=jnp.int32) // CAP
    col_group = slot_device % N_COL
    band_key, within_key = jax.random.split(key)
    band = jax.random.randint(band_key, (DEVICES * CAP,), 0, N_ROW, dtype=jnp.int32)
    within = jax.random.randint(within_key, (DEVICES * CAP,), 0, SB, dtype=jnp.int32)
    return (band * N_COL + col_group) * SB + within


def draw_live_counts(key, part):
    key = jax.random.fold_in(key, 37)
    count_key, top_key = jax.random.split(key)
    lowest = max(1, CAP // 8)
    counts = jax.random.randint(count_key, (DEVICES,), lowest, CAP // 2 + 1, dtype=jnp.int32)
    busiest = jax.random.randint(top_key, (), 0, DEVICES, dtype=jnp.int32)
    return jnp.where(jnp.arange(DEVICES, dtype=jnp.int32) == busiest, CAP, counts)


def block_scale(key, dims, pieces, smallest, top_value):
    factor_of = 1.0
    for position, shards_of in pieces:
        heights = jax.random.uniform(jax.random.fold_in(jax.random.fold_in(key, 6), position), (shards_of,), jnp.float32, smallest / len(pieces), top_value / len(pieces))
        factor_of = factor_of * jnp.repeat(jnp.exp(heights), dims[position] // shards_of).reshape((-1,) + (1,) * (len(dims) - 1 - position))
    return factor_of


def bell_draw(own_key, shape, deviation, limit, cuts=(), held_as=jnp.bfloat16):
    entries = jax.random.normal(own_key, shape, jnp.float32) * deviation
    if len(cuts) > 0:
        entries = block_scale(own_key, shape, cuts, -0.22, 0.18) * entries
    return jnp.clip(entries, min=-limit, max=limit).astype(held_as)


def setup_inputs(seed: int = 0) -> dict:
    arg_keys = jax.random.split(jax.random.key(seed), 6)
    vectors = bell_draw(arg_keys[0], (B * NV, NB), 1.0, 6.0, ((1, 128),), jnp.float32)
    blocks = bell_draw(arg_keys[1], (B * B, STORED), 0.05, 0.3, ((1, 128),), jnp.float32)
    blk_row = draw_blk_row(jax.random.fold_in(arg_keys[5], 71), 0)
    blk_col = draw_blk_col(jax.random.fold_in(arg_keys[5], 71), 0)
    live_counts = draw_live_counts(jax.random.fold_in(arg_keys[5], 71), 0)
    return dict(vectors=vectors, blocks=blocks, blk_row=blk_row, blk_col=blk_col, live_counts=live_counts)


def reference(vectors, blocks, blk_row, blk_col, live_counts):
    def visit_device(running, device):
        offset = device * CAP
        block_tile = lax.dynamic_slice_in_dim(blocks, offset, CAP, 1).reshape(B, B, CAP)
        rows_here = lax.dynamic_slice_in_dim(blk_row, offset, CAP, 0)
        cols_here = lax.dynamic_slice_in_dim(blk_col, offset, CAP, 0)
        live_mask = (jnp.arange(CAP, dtype=jnp.int32) < live_counts[device]).astype(blocks.dtype)
        source_cols = jnp.take(vectors, cols_here, axis=1).reshape(B, NV, CAP)
        source_rows = jnp.take(vectors, rows_here, axis=1).reshape(B, NV, CAP)
        plain_terms = jnp.einsum("ijg,jvg->ivg", block_tile, source_cols, precision=lax.Precision.HIGHEST)
        mirror_terms = jnp.einsum("jig,jvg->ivg", block_tile, source_rows, precision=lax.Precision.HIGHEST)
        plain_terms = plain_terms.reshape(B * NV, CAP) * live_mask
        mirror_terms = mirror_terms.reshape(B * NV, CAP) * live_mask
        running = running.at[:, rows_here].add(plain_terms)
        running = running.at[:, cols_here].add(mirror_terms)
        return running, None

    start_value = jnp.zeros((B * NV, NB), blocks.dtype)
    result, unused = lax.scan(visit_device, start_value, jnp.arange(DEVICES, dtype=jnp.int32))
    return result
```

```python
import functools

import jax
import jax.numpy as jnp
from jax import lax
from jax.experimental import pallas as pl
from jax.experimental.pallas import tpu as pltpu
from jax.sharding import PartitionSpec as P

MESH = pl.DeviceIdType.MESH
F32, BF16 = jnp.float32, jnp.bfloat16

B = 64
NV = 8
SB = 256
CAP = 1024
LANES = 128
NROW, NCOL = 8, 16
NZ = 4
HALF = NCOL // 2 * SB
RROWS = NCOL * SB
CROWS = NROW * SB
CHUNKS = 4
VC = NV // CHUNKS
FEAT = VC * B
GROUPS = CAP // LANES
PIECE = 2048
ROWS = RROWS + CROWS
DIRECT = ()

ORDER = (
    "R1.0", "C1.0", "R1.1", "R2.0", "C1.2", "C2.0", "C1.1", "R3a.0", "H.0", "R3b.0", "R2.1",
    "C3a.0", "R1.2", "C3b.0", "R1.3", "C2.2", "R3a.1", "C3a.1", "R4.0", "C2.1", "C1.3", "G1.0",
    "R3b.1", "R5.0", "C3a.2", "R2.2", "C4.0", "G2.0", "V.0", "T.0", "R3a.3", "C3b.1", "S1.0",
    "R3a.2", "R4.1", "C2.3", "R2.3", "G1.1", "S3.0", "S2.0", "R3b.2", "R5.1", "C3b.2", "D2.0",
    "C4.1", "G2.1", "V.1", "R3b.3", "E2b.0", "D3b.0", "T.1", "C3b.3", "R4.2", "E2a.0", "S1.1",
    "S3.1", "G1.2", "S2.1", "R4.3", "C4.2", "E3.0", "R5.2", "D3a.0", "G2.2", "D2.1", "C3a.3",
    "D3.0", "V.2", "D4.0", "E2a.1", "D3b.1", "E4.0", "T.2", "D3a.1", "E2b.1", "G1.3", "F.0", "S1.2",
    "S3.2", "S2.2", "E3.1", "D2.2", "D3.1", "D4.1", "C4.3", "E4.1", "R5.3", "G2.3", "V.3", "E2b.2",
    "T.3", "F.1", "D3b.2", "S1.3", "S2.3", "S3.3", "E3.2", "D2.3", "E2a.2", "D3a.2", "E2b.3",
    "D3a.3", "E2a.3", "D3.2", "D3b.3", "E3.3", "D4.2", "E4.2", "D3.3", "F.2", "E4.3", "D4.3", "F.3",
)


def split(x):
    hi = x.astype(BF16)
    lo = (x - hi.astype(F32)).astype(BF16)
    return jnp.concatenate([hi, lo], axis=0)


def places(rows, cols, live_total):
    here = rows - lax.axis_index("row") * RROWS
    strip = here // SB
    r_place = (strip % 2 * (NCOL // 2) + strip // 2) * SB + here % SB
    c_place = cols // RROWS * SB + cols % SB
    number = lax.broadcasted_iota(jnp.int32, rows.shape, 0) * LANES
    number = number + lax.broadcasted_iota(jnp.int32, rows.shape, 1)
    live = number < live_total
    return jnp.where(live, r_place, -1), jnp.where(live, c_place, -1)


def one_hots(place, first, rows, hot_ref):
    tile = 512

    def step(n, carry):
        start = pl.multiple_of(n * tile, tile)
        number = lax.broadcasted_iota(jnp.int32, (tile, LANES), 0) + start
        for q in range(GROUPS):
            hit = jnp.where(number == place[q : q + 1, :], 1.0, 0.0).astype(BF16)
            hot_ref[pl.ds(first + start, tile), q * LANES : (q + 1) * LANES] = hit
        return carry

    lax.fori_loop(0, rows // tile, step, 0)


def gather(x_ref, c, start, hot_ref):
    rows = pl.ds(pl.multiple_of(start, PIECE), PIECE)
    found = jnp.dot(split(x_ref[c, :, rows]), hot_ref[rows, :], preferred_element_type=F32)
    return found[:FEAT] + found[FEAT:]


def scatter(pt_ref, kind, start, hot_ref, out_ref, b):
    rows = pl.ds(pl.multiple_of(start, PIECE), PIECE)
    total = jnp.dot(hot_ref[rows, :], pt_ref[kind], preferred_element_type=F32)
    out_ref[b, rows, :] = total[:, :FEAT] + total[:, FEAT:]


def multiply(k_ref, g_ref, part_ref):
    tiles = B // 8

    def group(g, carry):
        cols = pl.ds(pl.multiple_of(g * LANES, LANES), LANES)
        x = [
            [g_ref[1, v * B + 8 * t : v * B + 8 * t + 8, cols] for t in range(tiles)]
            for v in range(VC)
        ]

        def rows(i, acc):
            acc = list(acc)
            mirror = [
                g_ref[0, v * B + i * 8 : v * B + i * 8 + 8, cols] for v in range(VC)
            ]
            for u in range(8):
                line = i * 8 + u
                k = [
                    k_ref[g, line * B + 8 * t : line * B + 8 * t + 8, :] for t in range(tiles)
                ]
                for v in range(VC):
                    plain = [k[t] * x[v][t] for t in range(tiles)]
                    while len(plain) > 1:
                        plain = [p + q for p, q in zip(plain[::2], plain[1::2])]
                    part_ref[v, line * 8 : line * 8 + 8, :] = plain[0]
                    other = jnp.broadcast_to(mirror[v][u : u + 1], (8, LANES))
                    for t in range(tiles):
                        acc[v * tiles + t] = acc[v * tiles + t] + k[t] * other
            return acc

        acc = [jnp.zeros((8, LANES), F32) for _ in range(VC * tiles)]
        for i in range(B // 8):
            acc = rows(i, acc)
        for v in range(VC):
            for t in range(tiles):
                here = slice(v * B + 8 * t, v * B + 8 * t + 8)
                g_ref[1, here, cols] = acc[v * tiles + t]
                total = part_ref[v, pl.ds(t * 64, 8, stride=8), :]
                for q in range(1, 8):
                    total = total + part_ref[v, pl.ds(t * 64 + q, 8, stride=8), :]
                g_ref[0, here, cols] = total
        return carry

    lax.fori_loop(0, GROUPS, group, 0)


def kernel(
    vec_ref,
    blk_ref,
    brow_ref,
    bcol_ref,
    live_ref,
    out_ref,
    k_ref,
    x_ref,
    hot_ref,
    p_ref,
    half_ref,
    rb_ref,
    cb_ref,
    g_ref,
    pt_ref,
    part_ref,
    res_ref,
    k_sem,
    v_sem,
    a_send,
    a_row,
    a_col,
    b_send,
    b_row,
    b_col,
    free_sem,
):
    row, col = lax.axis_index("row"), lax.axis_index("col")
    y, xl = row // 2, row % 2
    core, z, xh = col % 2, (col // 2) % NZ, col // 8
    yp, ym, y2 = (y + 1) % NZ, (y + 3) % NZ, (y + 2) % NZ
    zp, zm, z2 = (z + 1) % NZ, (z + 3) % NZ, (z + 2) % NZ

    def at(h, q):
        return (h * NZ + q) * 2 + core

    XH = dict(row=row, col=at(1 - xh, z))
    ZP = dict(row=row, col=at(xh, zp))
    ZM = dict(row=row, col=at(xh, zm))
    Z2 = dict(row=row, col=at(xh, z2))
    SIB = dict(row=row, col=(xh * NZ + z) * 2 + 1 - core)
    XL = dict(row=y * 2 + 1 - xl, col=col)
    YP = dict(row=yp * 2 + xl, col=col)
    YM = dict(row=ym * 2 + xl, col=col)
    Y2 = dict(row=y2 * 2 + xl, col=col)

    def strip(p):
        return pl.ds(pl.multiple_of(p * SB, SB), SB)

    def rstrip(h, q):
        return strip(core * 8 + h * NZ + q)

    def cstrip(q, l):
        return strip(NCOL + q * 2 + l)

    def half(k):
        return pl.ds(pl.multiple_of(k * HALF, HALF), HALF)

    vec_in = [
        pltpu.make_async_copy(
            vec_ref.at[:, h * LANES : (h + 1) * LANES], part_ref.at[h], v_sem.at[h]
        )
        for h in range(2)
    ]
    for load in vec_in:
        load.start()
    loads = [
        pltpu.make_async_copy(
            blk_ref.at[:, g * LANES : (g + 1) * LANES], k_ref.at[g], k_sem.at[g]
        )
        for g in range(GROUPS)
    ]
    for load in loads:
        load.start()

    barrier = pltpu.get_barrier_semaphore()
    for peer in (XH, ZP, ZM, Z2, SIB, XL, YP, YM, Y2):
        pl.semaphore_signal(barrier, inc=1, device_id=peer, device_id_type=MESH)

    for load in vec_in:
        load.wait()
    for c in range(CHUNKS):
        for v in range(VC):
            for h in range(2):
                x = part_ref[h, pl.ds(c * VC + v, B, stride=NV), :]
                for p in (core * 8 + xh * NZ + z, NCOL + row):
                    lanes = pl.ds(pl.multiple_of(p * SB + h * LANES, LANES), LANES)
                    x_ref[c, v * B : (v + 1) * B, lanes] = x

    pl.semaphore_wait(barrier, 9)

    def copy(src, dst, send, recv, peer):
        return pltpu.make_async_remote_copy(
            src_ref=src,
            dst_ref=dst,
            send_sem=send,
            recv_sem=recv,
            device_id=peer,
            device_id_type=MESH,
        )

    def a_r(c, n, h, q, peer):
        part = x_ref.at[c, :, rstrip(h, q)]
        return copy(part, part, a_send.at[c, n], a_row.at[c, h * NZ + q], peer)

    def a_c(c, n, q, l, peer):
        part = x_ref.at[c, :, cstrip(q, l)]
        return copy(part, part, a_send.at[c, n], a_col.at[c, q * 2 + l], peer)

    def a_half(c, k):
        part = x_ref.at[c, :, half(k)]
        return copy(part, part, a_send.at[c, 14], a_row.at[c, 8], SIB)

    def b_r(c, n, h, q, peer):
        src = p_ref.at[c % 2, rstrip(h, q), :]
        return copy(src, rb_ref.at[c, n], b_send.at[c, n], b_row.at[c, n], peer)

    def b_c(c, n, q, l, peer):
        src = p_ref.at[c % 2, cstrip(q, l), :]
        return copy(src, cb_ref.at[c, n], b_send.at[c, 8 + n], b_col.at[c, n], peer)

    def b_half(c):
        src = p_ref.at[c % 2, half(1 - core), :]
        return copy(src, half_ref.at[c % 2], b_send.at[c, 7], b_row.at[c, 7], SIB)

    def add(c, here, arrived, *slots):
        total = p_ref[c % 2, here, :]
        for n in slots:
            total = total + arrived[c, n]
        p_ref[c % 2, here, :] = total

    def out_r(c, n):
        to = (
            (xh, z2, ZP),
            (1 - xh, z2, ZM),
            (1 - xh, zp, ZP),
            (xh, zm, ZM),
            (xh, zp, ZP),
            (1 - xh, zm, ZM),
            (1 - xh, z, XH),
        )
        return b_r(c, n, *to[n])

    def out_c(c, n):
        to = (
            (y2, xl, YP),
            (y2, 1 - xl, YM),
            (yp, 1 - xl, YP),
            (ym, xl, YM),
            (yp, xl, YP),
            (ym, 1 - xl, YM),
            (y, 1 - xl, XL),
        )
        return b_c(c, n, *to[n])

    def H(c):
        r_place, c_place = places(brow_ref[...], bcol_ref[...], live_ref[0])
        one_hots(r_place, 0, RROWS, hot_ref)
        one_hots(c_place, RROWS, CROWS, hot_ref)

    def R1(c):
        a_r(c, 0, xh, z, XH).start()
        a_r(c, 1, xh, z, ZP).start()
        a_r(c, 2, xh, z, ZM).start()
        if c in DIRECT:
            a_r(c, 5, xh, z, Z2).start()

    def C1(c):
        a_c(c, 7, y, xl, XL).start()
        a_c(c, 8, y, xl, YP).start()
        a_c(c, 9, y, xl, YM).start()
        if c in DIRECT:
            a_c(c, 12, y, xl, Y2).start()

    def R2(c):
        a_r(c, 0, 1 - xh, z, XH).wait_recv()
        a_r(c, 3, 1 - xh, z, ZP).start()
        a_r(c, 4, 1 - xh, z, ZM).start()
        if c in DIRECT:
            a_r(c, 6, 1 - xh, z, Z2).start()

    def C2(c):
        a_c(c, 7, y, 1 - xl, XL).wait_recv()
        a_c(c, 10, y, 1 - xl, YP).start()
        a_c(c, 11, y, 1 - xl, YM).start()
        if c in DIRECT:
            a_c(c, 13, y, 1 - xl, Y2).start()

    def R3a(c):
        a_r(c, 0, xh, zp, ZP).wait_recv()
        a_r(c, 5, xh, zp, ZM).start()

    def R3b(c):
        a_r(c, 0, 1 - xh, zm, ZM).wait_recv()
        a_r(c, 6, 1 - xh, zm, ZP).start()

    def C3a(c):
        a_c(c, 7, yp, xl, YP).wait_recv()
        a_c(c, 12, yp, xl, YM).start()

    def C3b(c):
        a_c(c, 7, ym, 1 - xl, YM).wait_recv()
        a_c(c, 13, ym, 1 - xl, YP).start()

    def R4(c):
        if c in DIRECT:
            a_r(c, 0, xh, zp, ZP).wait_recv()
            a_r(c, 0, 1 - xh, zm, ZM).wait_recv()
        for h, q in ((xh, zm), (1 - xh, zp), (xh, z2), (1 - xh, z2)):
            a_r(c, 0, h, q, ZP).wait_recv()
        a_half(c, core).start()

    def C4(c):
        if c in DIRECT:
            a_c(c, 7, yp, xl, YP).wait_recv()
            a_c(c, 7, ym, 1 - xl, YM).wait_recv()
        for q, l in ((ym, xl), (yp, 1 - xl), (y2, xl), (y2, 1 - xl)):
            a_c(c, 7, q, l, YP).wait_recv()

    def R5(c):
        a_half(c, 1 - core).wait_recv()

    def G1(c):
        g_ref[0] = gather(x_ref, c, core * HALF, hot_ref)
        g_ref[1] = jnp.zeros((FEAT, CAP), F32)

    def G2(c):
        def step(kind, carry):
            start = (1 - kind) * (1 - core) * HALF + kind * RROWS
            g_ref[kind] = g_ref[kind] + gather(x_ref, c, start, hot_ref)
            return carry

        lax.fori_loop(0, 2, step, 0)

    def V(c):
        if c == 0:
            for load in loads:
                load.wait()
        multiply(k_ref, g_ref, part_ref)

    def T(c):
        for kind in range(2):
            p = jnp.transpose(g_ref[kind])
            hi = p.astype(BF16)
            pt_ref[kind, :, :FEAT] = hi
            pt_ref[kind, :, FEAT:] = (p - hi.astype(F32)).astype(BF16)

    def sent(c):
        b_half(c).wait_send()
        for n in range(7):
            out_r(c, n).wait_send()
            out_c(c, n).wait_send()

    def S1(c):
        if c >= 2:
            sent(c - 2)
            pl.semaphore_wait(free_sem, 1)
        scatter(pt_ref, 0, (1 - core) * HALF, hot_ref, p_ref, c % 2)
        b_half(c).start()

    def S2(c):
        scatter(pt_ref, 1, RROWS, hot_ref, p_ref, c % 2)
        for n in range(4):
            out_c(c, n).start()

    def S3(c):
        scatter(pt_ref, 0, core * HALF, hot_ref, p_ref, c % 2)

    def D2(c):
        b_half(c).wait_recv()
        p_ref[c % 2, half(core), :] = p_ref[c % 2, half(core), :] + half_ref[c % 2]
        if c + 2 < CHUNKS:
            pl.semaphore_signal(free_sem, inc=1, device_id=SIB, device_id_type=MESH)
        for n in range(4):
            out_r(c, n).start()

    def E2a(c):
        out_c(c, 0).wait_recv()
        add(c, cstrip(yp, xl), cb_ref, 0)
        out_c(c, 4).start()

    def E2b(c):
        out_c(c, 1).wait_recv()
        add(c, cstrip(ym, 1 - xl), cb_ref, 1)
        out_c(c, 5).start()

    def D3a(c):
        out_r(c, 0).wait_recv()
        add(c, rstrip(xh, zp), rb_ref, 0)
        out_r(c, 4).start()

    def D3b(c):
        out_r(c, 1).wait_recv()
        add(c, rstrip(1 - xh, zm), rb_ref, 1)
        out_r(c, 5).start()

    def E3(c):
        for n in (2, 5):
            out_c(c, n).wait_recv()
        add(c, cstrip(y, 1 - xl), cb_ref, 2, 5)
        out_c(c, 6).start()

    def D3(c):
        for n in (2, 5):
            out_r(c, n).wait_recv()
        add(c, rstrip(1 - xh, z), rb_ref, 2, 5)
        out_r(c, 6).start()

    def E4(c):
        for n in (3, 4):
            out_c(c, n).wait_recv()
        add(c, cstrip(y, xl), cb_ref, 3, 4)

    def D4(c):
        for n in (3, 4):
            out_r(c, n).wait_recv()
        add(c, rstrip(xh, z), rb_ref, 3, 4)

    def F(c):
        out_r(c, 6).wait_recv()
        out_c(c, 6).wait_recv()
        total = p_ref[c % 2, rstrip(xh, z), :] + rb_ref[c, 6]
        total = total + (p_ref[c % 2, cstrip(y, xl), :] + cb_ref[c, 6])
        total = jnp.transpose(total)
        for v in range(VC):
            for h in range(2):
                res_ref[h, pl.ds(c * VC + v, B, stride=NV), :] = total[
                    v * B : (v + 1) * B, h * LANES : (h + 1) * LANES
                ]

    steps = dict(R1=R1, C1=C1, R2=R2, C2=C2, R3a=R3a, R3b=R3b, C3a=C3a, C3b=C3b, R4=R4, C4=C4)
    steps.update(R5=R5, G1=G1, G2=G2, V=V, T=T, S1=S1, S2=S2, S3=S3, D2=D2, E2a=E2a, E2b=E2b)
    steps.update(D3a=D3a, D3b=D3b, E3=E3, D3=D3, E4=E4, D4=D4, F=F)
    steps.update(H=H)
    for step in ORDER:
        name, c = step.split(".")
        steps[name](int(c))

    results = [
        pltpu.make_async_copy(
            res_ref.at[h], out_ref.at[:, h * LANES : (h + 1) * LANES], v_sem.at[h]
        )
        for h in range(2)
    ]
    for store in results:
        store.start()
    for c in range(CHUNKS):
        for n in range(7):
            a_r(c, n, xh, z, XH).wait_send()
            a_c(c, 7 + n, y, xl, XL).wait_send()
        a_half(c, core).wait_send()
    for c in range(max(0, CHUNKS - 2), CHUNKS):
        sent(c)
    for store in results:
        store.wait()


def body(vectors, blocks, blk_row, blk_col, live_counts):
    vmem = pl.BlockSpec(memory_space=pltpu.VMEM)
    hbm = pl.BlockSpec(memory_space=pl.ANY)
    dma = pltpu.SemaphoreType.DMA
    return pl.pallas_call(
        kernel,
        out_shape=jax.ShapeDtypeStruct((B * NV, SB), F32),
        in_specs=[hbm, hbm, vmem, vmem, pl.BlockSpec(memory_space=pltpu.SMEM)],
        out_specs=hbm,
        scratch_shapes=[
            pltpu.VMEM((GROUPS, B * B, LANES), F32),
            pltpu.VMEM((CHUNKS, FEAT, ROWS), F32),
            pltpu.VMEM((ROWS, CAP), BF16),
            pltpu.VMEM((2, ROWS, FEAT), F32),
            pltpu.VMEM((2, HALF, FEAT), F32),
            pltpu.VMEM((CHUNKS, 7, SB, FEAT), F32),
            pltpu.VMEM((CHUNKS, 7, SB, FEAT), F32),
            pltpu.VMEM((2, FEAT, CAP), F32),
            pltpu.VMEM((2, CAP, 2 * FEAT), BF16),
            pltpu.VMEM((2, B * NV, LANES), F32),
            pltpu.VMEM((2, B * NV, LANES), F32),
            dma((GROUPS,)),
            dma((2,)),
            dma((CHUNKS, 15)),
            dma((CHUNKS, 9)),
            dma((CHUNKS, 8)),
            dma((CHUNKS, 15)),
            dma((CHUNKS, 8)),
            dma((CHUNKS, 7)),
            pltpu.SemaphoreType.REGULAR,
        ],
        compiler_params=pltpu.CompilerParams(
            collective_id=0, has_side_effects=True, vmem_limit_bytes=63 * 2**20
        ),
        name="block_product",
    )(vectors, blocks, blk_row.reshape(GROUPS, LANES), blk_col.reshape(GROUPS, LANES), live_counts)


def solution(mesh):
    return jax.shard_map(
        body,
        mesh=mesh,
        in_specs=(
            P(None, ("row", "col")),
            P(None, ("row", "col")),
            P(("row", "col")),
            P(("row", "col")),
            P(("row", "col")),
        ),
        out_specs=P(None, ("row", "col")),
        check_vma=False,
    )
```

```python
import functools

import jax
import jax.numpy as jnp
from jax import lax
from jax.experimental import pallas as pl
from jax.experimental.pallas import tpu as pltpu
from jax.sharding import PartitionSpec as P

MESH = pl.DeviceIdType.MESH
F32, BF16 = jnp.float32, jnp.bfloat16

B = 64
NV = 8
SB = 256
CAP = 1024
LANES = 128
NROW, NCOL = 8, 16
NZ = 4
HALF = NCOL // 2 * SB
RROWS = NCOL * SB
CROWS = NROW * SB
CHUNKS = 4
VC = NV // CHUNKS
FEAT = VC * B
GROUPS = CAP // LANES
PIECE = 2048
ROWS = RROWS + CROWS
DIRECT = ()

ORDER = (
    "R1.0", "C1.0", "R1.1", "R2.0", "C1.2", "C2.0", "C1.1", "R3a.0", "R3b.0", "R2.1",
    "C3a.0", "R1.2", "C3b.0", "R1.3", "C2.2", "R3a.1", "C3a.1", "R4.0", "C2.1", "C1.3", "G1.0",
    "R3b.1", "R5.0", "C3a.2", "R2.2", "C4.0", "G2.0", "V.0", "T.0", "R3a.3", "C3b.1", "S1.0",
    "R3a.2", "R4.1", "C2.3", "R2.3", "G1.1", "S3.0", "S2.0", "R3b.2", "R5.1", "C3b.2", "D2.0",
    "C4.1", "G2.1", "V.1", "R3b.3", "E2b.0", "D3b.0", "T.1", "C3b.3", "R4.2", "E2a.0", "S1.1",
    "S3.1", "G1.2", "S2.1", "R4.3", "C4.2", "E3.0", "R5.2", "D3a.0", "G2.2", "D2.1", "C3a.3",
    "D3.0", "V.2", "D4.0", "E2a.1", "D3b.1", "E4.0", "T.2", "D3a.1", "E2b.1", "G1.3", "F.0", "S1.2",
    "S3.2", "S2.2", "E3.1", "D2.2", "D3.1", "D4.1", "C4.3", "E4.1", "R5.3", "G2.3", "V.3", "E2b.2",
    "T.3", "F.1", "D3b.2", "S1.3", "S2.3", "S3.3", "E3.2", "D2.3", "E2a.2", "D3a.2", "E2b.3",
    "D3a.3", "E2a.3", "D3.2", "D3b.3", "E3.3", "D4.2", "E4.2", "D3.3", "F.2", "E4.3", "D4.3", "F.3",
)


def split(x):
    hi = x.astype(BF16)
    lo = (x - hi.astype(F32)).astype(BF16)
    return jnp.concatenate([hi, lo], axis=0)


def places(rows, cols, live_total):
    here = rows - lax.axis_index("row") * RROWS
    strip = here // SB
    r_place = (strip % 2 * (NCOL // 2) + strip // 2) * SB + here % SB
    c_place = cols // RROWS * SB + cols % SB
    number = lax.broadcasted_iota(jnp.int32, rows.shape, 0) * LANES
    number = number + lax.broadcasted_iota(jnp.int32, rows.shape, 1)
    live = number < live_total
    return jnp.where(live, r_place, -1), jnp.where(live, c_place, -1)


def one_hots(place, first, rows, hot_ref):
    tile = 512

    def step(n, carry):
        start = pl.multiple_of(n * tile, tile)
        number = lax.broadcasted_iota(jnp.int32, (tile, LANES), 0) + start
        for q in range(GROUPS):
            hit = jnp.where(number == place[q : q + 1, :], 1.0, 0.0).astype(BF16)
            hot_ref[pl.ds(first + start, tile), q * LANES : (q + 1) * LANES] = hit
        return carry

    lax.fori_loop(0, rows // tile, step, 0)


def gather(x_ref, c, start, hot_ref):
    rows = pl.ds(pl.multiple_of(start, PIECE), PIECE)
    found = jnp.dot(split(x_ref[c, :, rows]), hot_ref[rows, :], preferred_element_type=F32)
    return found[:FEAT] + found[FEAT:]


def scatter(pt_ref, kind, start, hot_ref, out_ref, b):
    rows = pl.ds(pl.multiple_of(start, PIECE), PIECE)
    total = jnp.dot(hot_ref[rows, :], pt_ref[kind], preferred_element_type=F32)
    out_ref[b, rows, :] = total[:, :FEAT] + total[:, FEAT:]


def multiply(k_ref, g_ref, part_ref):
    tiles = B // 8

    def group(g, carry):
        cols = pl.ds(pl.multiple_of(g * LANES, LANES), LANES)
        x = [
            [g_ref[1, v * B + 8 * t : v * B + 8 * t + 8, cols] for t in range(tiles)]
            for v in range(VC)
        ]

        def rows(i, acc):
            acc = list(acc)
            mirror = [
                g_ref[0, v * B + i * 8 : v * B + i * 8 + 8, cols] for v in range(VC)
            ]
            for u in range(8):
                line = i * 8 + u
                k = [
                    k_ref[g, line * B + 8 * t : line * B + 8 * t + 8, :] for t in range(tiles)
                ]
                for v in range(VC):
                    plain = [k[t] * x[v][t] for t in range(tiles)]
                    while len(plain) > 1:
                        plain = [p + q for p, q in zip(plain[::2], plain[1::2])]
                    part_ref[v, line * 8 : line * 8 + 8, :] = plain[0]
                    other = jnp.broadcast_to(mirror[v][u : u + 1], (8, LANES))
                    for t in range(tiles):
                        acc[v * tiles + t] = acc[v * tiles + t] + k[t] * other
            return acc

        acc = [jnp.zeros((8, LANES), F32) for _ in range(VC * tiles)]
        for i in range(B // 8):
            acc = rows(i, acc)
        for v in range(VC):
            for t in range(tiles):
                here = slice(v * B + 8 * t, v * B + 8 * t + 8)
                g_ref[1, here, cols] = acc[v * tiles + t]
                total = part_ref[v, pl.ds(t * 64, 8, stride=8), :]
                for q in range(1, 8):
                    total = total + part_ref[v, pl.ds(t * 64 + q, 8, stride=8), :]
                g_ref[0, here, cols] = total
        return carry

    lax.fori_loop(0, GROUPS, group, 0)


def kernel(
    vec_ref,
    blk_ref,
    brow_ref,
    bcol_ref,
    live_ref,
    out_ref,
    k_ref,
    x_ref,
    hot_ref,
    p_ref,
    half_ref,
    rb_ref,
    cb_ref,
    g_ref,
    pt_ref,
    part_ref,
    res_ref,
    k_sem,
    v_sem,
    a_send,
    a_row,
    a_col,
    b_send,
    b_row,
    b_col,
    free_sem,
):
    row, col = lax.axis_index("row"), lax.axis_index("col")
    y, xl = row // 2, row % 2
    core, z, xh = col % 2, (col // 2) % NZ, col // 8
    yp, ym, y2 = (y + 1) % NZ, (y + 3) % NZ, (y + 2) % NZ
    zp, zm, z2 = (z + 1) % NZ, (z + 3) % NZ, (z + 2) % NZ

    def at(h, q):
        return (h * NZ + q) * 2 + core

    XH = dict(row=row, col=at(1 - xh, z))
    ZP = dict(row=row, col=at(xh, zp))
    ZM = dict(row=row, col=at(xh, zm))
    Z2 = dict(row=row, col=at(xh, z2))
    SIB = dict(row=row, col=(xh * NZ + z) * 2 + 1 - core)
    XL = dict(row=y * 2 + 1 - xl, col=col)
    YP = dict(row=yp * 2 + xl, col=col)
    YM = dict(row=ym * 2 + xl, col=col)
    Y2 = dict(row=y2 * 2 + xl, col=col)

    def strip(p):
        return pl.ds(pl.multiple_of(p * SB, SB), SB)

    def rstrip(h, q):
        return strip(core * 8 + h * NZ + q)

    def cstrip(q, l):
        return strip(NCOL + q * 2 + l)

    def half(k):
        return pl.ds(pl.multiple_of(k * HALF, HALF), HALF)

    vec_in = [
        pltpu.make_async_copy(
            vec_ref.at[:, h * LANES : (h + 1) * LANES], part_ref.at[h], v_sem.at[h]
        )
        for h in range(2)
    ]
    for load in vec_in:
        load.start()
    loads = [
        pltpu.make_async_copy(
            blk_ref.at[:, g * LANES : (g + 1) * LANES], k_ref.at[g], k_sem.at[g]
        )
        for g in range(GROUPS)
    ]
    for load in loads:
        load.start()

    barrier = pltpu.get_barrier_semaphore()
    for peer in (XH, ZP, ZM, Z2, SIB, XL, YP, YM, Y2):
        pl.semaphore_signal(barrier, inc=1, device_id=peer, device_id_type=MESH)

    for load in vec_in:
        load.wait()
    for c in range(CHUNKS):
        for v in range(VC):
            for h in range(2):
                x = part_ref[h, pl.ds(c * VC + v, B, stride=NV), :]
                for p in (core * 8 + xh * NZ + z, NCOL + row):
                    lanes = pl.ds(pl.multiple_of(p * SB + h * LANES, LANES), LANES)
                    x_ref[c, v * B : (v + 1) * B, lanes] = x

    r_place, c_place = places(brow_ref[...], bcol_ref[...], live_ref[0])
    one_hots(r_place, 0, RROWS, hot_ref)
    one_hots(c_place, RROWS, CROWS, hot_ref)
    pl.semaphore_wait(barrier, 9)

    def copy(src, dst, send, recv, peer):
        return pltpu.make_async_remote_copy(
            src_ref=src,
            dst_ref=dst,
            send_sem=send,
            recv_sem=recv,
            device_id=peer,
            device_id_type=MESH,
        )

    def a_r(c, n, h, q, peer):
        part = x_ref.at[c, :, rstrip(h, q)]
        return copy(part, part, a_send.at[c, n], a_row.at[c, h * NZ + q], peer)

    def a_c(c, n, q, l, peer):
        part = x_ref.at[c, :, cstrip(q, l)]
        return copy(part, part, a_send.at[c, n], a_col.at[c, q * 2 + l], peer)

    def a_half(c, k):
        part = x_ref.at[c, :, half(k)]
        return copy(part, part, a_send.at[c, 14], a_row.at[c, 8], SIB)

    def b_r(c, n, h, q, peer):
        src = p_ref.at[c % 2, rstrip(h, q), :]
        return copy(src, rb_ref.at[c, n], b_send.at[c, n], b_row.at[c, n], peer)

    def b_c(c, n, q, l, peer):
        src = p_ref.at[c % 2, cstrip(q, l), :]
        return copy(src, cb_ref.at[c, n], b_send.at[c, 8 + n], b_col.at[c, n], peer)

    def b_half(c):
        src = p_ref.at[c % 2, half(1 - core), :]
        return copy(src, half_ref.at[c % 2], b_send.at[c, 7], b_row.at[c, 7], SIB)

    def add(c, here, arrived, *slots):
        total = p_ref[c % 2, here, :]
        for n in slots:
            total = total + arrived[c, n]
        p_ref[c % 2, here, :] = total

    def out_r(c, n):
        to = (
            (xh, z2, ZP),
            (1 - xh, z2, ZM),
            (1 - xh, zp, ZP),
            (xh, zm, ZM),
            (xh, zp, ZP),
            (1 - xh, zm, ZM),
            (1 - xh, z, XH),
        )
        return b_r(c, n, *to[n])

    def out_c(c, n):
        to = (
            (y2, xl, YP),
            (y2, 1 - xl, YM),
            (yp, 1 - xl, YP),
            (ym, xl, YM),
            (yp, xl, YP),
            (ym, 1 - xl, YM),
            (y, 1 - xl, XL),
        )
        return b_c(c, n, *to[n])

    def R1(c):
        a_r(c, 0, xh, z, XH).start()
        a_r(c, 1, xh, z, ZP).start()
        a_r(c, 2, xh, z, ZM).start()
        if c in DIRECT:
            a_r(c, 5, xh, z, Z2).start()

    def C1(c):
        a_c(c, 7, y, xl, XL).start()
        a_c(c, 8, y, xl, YP).start()
        a_c(c, 9, y, xl, YM).start()
        if c in DIRECT:
            a_c(c, 12, y, xl, Y2).start()

    def R2(c):
        a_r(c, 0, 1 - xh, z, XH).wait_recv()
        a_r(c, 3, 1 - xh, z, ZP).start()
        a_r(c, 4, 1 - xh, z, ZM).start()
        if c in DIRECT:
            a_r(c, 6, 1 - xh, z, Z2).start()

    def C2(c):
        a_c(c, 7, y, 1 - xl, XL).wait_recv()
        a_c(c, 10, y, 1 - xl, YP).start()
        a_c(c, 11, y, 1 - xl, YM).start()
        if c in DIRECT:
            a_c(c, 13, y, 1 - xl, Y2).start()

    def R3a(c):
        a_r(c, 0, xh, zp, ZP).wait_recv()
        a_r(c, 5, xh, zp, ZM).start()

    def R3b(c):
        a_r(c, 0, 1 - xh, zm, ZM).wait_recv()
        a_r(c, 6, 1 - xh, zm, ZP).start()

    def C3a(c):
        a_c(c, 7, yp, xl, YP).wait_recv()
        a_c(c, 12, yp, xl, YM).start()

    def C3b(c):
        a_c(c, 7, ym, 1 - xl, YM).wait_recv()
        a_c(c, 13, ym, 1 - xl, YP).start()

    def R4(c):
        if c in DIRECT:
            a_r(c, 0, xh, zp, ZP).wait_recv()
            a_r(c, 0, 1 - xh, zm, ZM).wait_recv()
        for h, q in ((xh, zm), (1 - xh, zp), (xh, z2), (1 - xh, z2)):
            a_r(c, 0, h, q, ZP).wait_recv()
        a_half(c, core).start()

    def C4(c):
        if c in DIRECT:
            a_c(c, 7, yp, xl, YP).wait_recv()
            a_c(c, 7, ym, 1 - xl, YM).wait_recv()
        for q, l in ((ym, xl), (yp, 1 - xl), (y2, xl), (y2, 1 - xl)):
            a_c(c, 7, q, l, YP).wait_recv()

    def R5(c):
        a_half(c, 1 - core).wait_recv()

    def G1(c):
        g_ref[0] = gather(x_ref, c, core * HALF, hot_ref)
        g_ref[1] = jnp.zeros((FEAT, CAP), F32)

    def G2(c):
        def step(kind, carry):
            start = (1 - kind) * (1 - core) * HALF + kind * RROWS
            g_ref[kind] = g_ref[kind] + gather(x_ref, c, start, hot_ref)
            return carry

        lax.fori_loop(0, 2, step, 0)

    def V(c):
        if c == 0:
            for load in loads:
                load.wait()
        multiply(k_ref, g_ref, part_ref)

    def T(c):
        for kind in range(2):
            p = jnp.transpose(g_ref[kind])
            hi = p.astype(BF16)
            pt_ref[kind, :, :FEAT] = hi
            pt_ref[kind, :, FEAT:] = (p - hi.astype(F32)).astype(BF16)

    def sent(c):
        b_half(c).wait_send()
        for n in range(7):
            out_r(c, n).wait_send()
            out_c(c, n).wait_send()

    def S1(c):
        if c >= 2:
            sent(c - 2)
            pl.semaphore_wait(free_sem, 1)
        scatter(pt_ref, 0, (1 - core) * HALF, hot_ref, p_ref, c % 2)
        b_half(c).start()

    def S2(c):
        scatter(pt_ref, 1, RROWS, hot_ref, p_ref, c % 2)
        for n in range(4):
            out_c(c, n).start()

    def S3(c):
        scatter(pt_ref, 0, core * HALF, hot_ref, p_ref, c % 2)

    def D2(c):
        b_half(c).wait_recv()
        p_ref[c % 2, half(core), :] = p_ref[c % 2, half(core), :] + half_ref[c % 2]
        if c + 2 < CHUNKS:
            pl.semaphore_signal(free_sem, inc=1, device_id=SIB, device_id_type=MESH)
        for n in range(4):
            out_r(c, n).start()

    def E2a(c):
        out_c(c, 0).wait_recv()
        add(c, cstrip(yp, xl), cb_ref, 0)
        out_c(c, 4).start()

    def E2b(c):
        out_c(c, 1).wait_recv()
        add(c, cstrip(ym, 1 - xl), cb_ref, 1)
        out_c(c, 5).start()

    def D3a(c):
        out_r(c, 0).wait_recv()
        add(c, rstrip(xh, zp), rb_ref, 0)
        out_r(c, 4).start()

    def D3b(c):
        out_r(c, 1).wait_recv()
        add(c, rstrip(1 - xh, zm), rb_ref, 1)
        out_r(c, 5).start()

    def E3(c):
        for n in (2, 5):
            out_c(c, n).wait_recv()
        add(c, cstrip(y, 1 - xl), cb_ref, 2, 5)
        out_c(c, 6).start()

    def D3(c):
        for n in (2, 5):
            out_r(c, n).wait_recv()
        add(c, rstrip(1 - xh, z), rb_ref, 2, 5)
        out_r(c, 6).start()

    def E4(c):
        for n in (3, 4):
            out_c(c, n).wait_recv()
        add(c, cstrip(y, xl), cb_ref, 3, 4)

    def D4(c):
        for n in (3, 4):
            out_r(c, n).wait_recv()
        add(c, rstrip(xh, z), rb_ref, 3, 4)

    def F(c):
        out_r(c, 6).wait_recv()
        out_c(c, 6).wait_recv()
        total = p_ref[c % 2, rstrip(xh, z), :] + rb_ref[c, 6]
        total = total + (p_ref[c % 2, cstrip(y, xl), :] + cb_ref[c, 6])
        total = jnp.transpose(total)
        for v in range(VC):
            for h in range(2):
                res_ref[h, pl.ds(c * VC + v, B, stride=NV), :] = total[
                    v * B : (v + 1) * B, h * LANES : (h + 1) * LANES
                ]

    steps = dict(R1=R1, C1=C1, R2=R2, C2=C2, R3a=R3a, R3b=R3b, C3a=C3a, C3b=C3b, R4=R4, C4=C4)
    steps.update(R5=R5, G1=G1, G2=G2, V=V, T=T, S1=S1, S2=S2, S3=S3, D2=D2, E2a=E2a, E2b=E2b)
    steps.update(D3a=D3a, D3b=D3b, E3=E3, D3=D3, E4=E4, D4=D4, F=F)
    for step in ORDER:
        name, c = step.split(".")
        steps[name](int(c))

    results = [
        pltpu.make_async_copy(
            res_ref.at[h], out_ref.at[:, h * LANES : (h + 1) * LANES], v_sem.at[h]
        )
        for h in range(2)
    ]
    for store in results:
        store.start()
    for c in range(CHUNKS):
        for n in range(7):
            a_r(c, n, xh, z, XH).wait_send()
            a_c(c, 7 + n, y, xl, XL).wait_send()
        a_half(c, core).wait_send()
    for c in range(max(0, CHUNKS - 2), CHUNKS):
        sent(c)
    for store in results:
        store.wait()


def body(vectors, blocks, blk_row, blk_col, live_counts):
    vmem = pl.BlockSpec(memory_space=pltpu.VMEM)
    hbm = pl.BlockSpec(memory_space=pl.ANY)
    dma = pltpu.SemaphoreType.DMA
    return pl.pallas_call(
        kernel,
        out_shape=jax.ShapeDtypeStruct((B * NV, SB), F32),
        in_specs=[hbm, hbm, vmem, vmem, pl.BlockSpec(memory_space=pltpu.SMEM)],
        out_specs=hbm,
        scratch_shapes=[
            pltpu.VMEM((GROUPS, B * B, LANES), F32),
            pltpu.VMEM((CHUNKS, FEAT, ROWS), F32),
            pltpu.VMEM((ROWS, CAP), BF16),
            pltpu.VMEM((2, ROWS, FEAT), F32),
            pltpu.VMEM((2, HALF, FEAT), F32),
            pltpu.VMEM((CHUNKS, 7, SB, FEAT), F32),
            pltpu.VMEM((CHUNKS, 7, SB, FEAT), F32),
            pltpu.VMEM((2, FEAT, CAP), F32),
            pltpu.VMEM((2, CAP, 2 * FEAT), BF16),
            pltpu.VMEM((2, B * NV, LANES), F32),
            pltpu.VMEM((2, B * NV, LANES), F32),
            dma((GROUPS,)),
            dma((2,)),
            dma((CHUNKS, 15)),
            dma((CHUNKS, 9)),
            dma((CHUNKS, 8)),
            dma((CHUNKS, 15)),
            dma((CHUNKS, 8)),
            dma((CHUNKS, 7)),
            pltpu.SemaphoreType.REGULAR,
        ],
        compiler_params=pltpu.CompilerParams(
            collective_id=0, has_side_effects=True, vmem_limit_bytes=63 * 2**20
        ),
        name="block_product",
    )(vectors, blocks, blk_row.reshape(GROUPS, LANES), blk_col.reshape(GROUPS, LANES), live_counts)


def solution(mesh):
    return jax.shard_map(
        body,
        mesh=mesh,
        in_specs=(
            P(None, ("row", "col")),
            P(None, ("row", "col")),
            P(("row", "col")),
            P(("row", "col")),
            P(("row", "col")),
        ),
        out_specs=P(None, ("row", "col")),
        check_vma=False,
    )
```
